512 devices in a mesh: layer: 16 (over z_lo, x), latent: 32 (over z_hi, y, core).
Axes of the slice: x: 4, y: 4, z: 16 (z_hi: 4, z_lo: 4; z = z_hi * 4 + z_lo), core: 2. Of those that a mesh axis runs over, the one named last changes fastest.
Arguments:
- residual: bfloat16 [16, 512, 1024], P('layer', 'latent'), may hold values from -6 to 6
- targets: bfloat16 [16, 512, 1024], P('layer', 'latent'), may hold values from -6 to 6
- enc_weight: bfloat16 [16, 1024, 12288], P('layer', None, 'latent'), may hold values from -0.1875 to 0.1875
- enc_bias: float32 [16, 12288], P('layer', 'latent'), may hold values from -3 to 3
- dec_weight: bfloat16 [16, 2, 12288, 1024], P('layer', None, 'latent'), may hold values from -0.0390625 to 0.0390625
Outputs:
- recon: bfloat16 [16, 512, 1024], P('layer', 'latent')
- dec_grad: bfloat16 [16, 2, 12288, 1024], P('layer', None, 'latent')
- latent_grad: bfloat16 [16, 512, 12288], P('layer', None, 'latent')
The draws below stay inside these ranges and needn't reach their ends.
All inputs are finite; a program needn't handle non-finite values.
Results may differ from the reference program's by a relative error of at most 0.0053.
Values may be sent and summed in bfloat16 or wider, within the bound.
No kernel may reach another device: no remote copies, remote signals or barrier semaphores. Data moves between devices by JAX's collectives and lax.ppermute only.
A program may use at most 64 MiB of HBM per device.

```python
import jax
import jax.numpy as jnp

D = 1024
SPAN = 2
TOK = 512
LAYERS = 16
LATENTS = 12288


def level_of(own_key, dims, shards, low, high):
    loudness = 1.0
    for position, shards_of in shards:
        draws = jax.random.uniform(jax.random.fold_in(jax.random.fold_in(own_key, 6), position), (shards_of,), jnp.float32, low / len(shards), high / len(shards))
        loudness = loudness * jnp.repeat(jnp.exp(draws), dims[position] // shards_of).reshape((-1,) + (1,) * (len(dims) - 1 - position))
    return loudness


def bell_draw(rng, extent, spread, most, pieces=(), kind=jnp.bfloat16):
    entries = jax.random.normal(rng, extent, jnp.float32) * spread
    if len(pieces) > 0:
        entries = level_of(rng, extent, pieces, -0.22, 0.18) * entries
    return jnp.clip(entries, min=-most, max=most).astype(kind)


def setup_inputs(seed: int = 0) -> dict:
    key_of = jax.random.split(jax.random.key(seed), 6)
    residual = bell_draw(key_of[0], (LAYERS, TOK, D), 1.0, 6.0, ((0, 16), (1, 32)))
    targets = bell_draw(key_of[1], (LAYERS, TOK, D), 1.0, 6.0, ((0, 16), (1, 32)))
    enc_weight = bell_draw(key_of[2], (LAYERS, D, LATENTS), D ** -0.5, 0.1875, ((0, 16), (2, 32)))
    enc_bias = bell_draw(key_of[3], (LAYERS, LATENTS), 0.5, 3.0, ((0, 16), (1, 32)), jnp.float32)
    dec_weight = bell_draw(key_of[4], (LAYERS, SPAN, LATENTS, D), (LATENTS * SPAN) ** -0.5, 0.0390625, ((0, 16), (2, 32)))
    return dict(residual=residual, targets=targets, enc_weight=enc_weight, enc_bias=enc_bias, dec_weight=dec_weight)


def reference(residual, targets, enc_weight, enc_bias, dec_weight):
    latents = []
    for layer_idx in range(LAYERS):
        pre = jnp.dot(residual[layer_idx], enc_weight[layer_idx], preferred_element_type=jnp.float32) + enc_bias[layer_idx]
        latents.append(jax.nn.relu(pre).astype(jnp.bfloat16))
    recons = []
    errors = []
    for target in range(LAYERS):
        summed = jnp.zeros((TOK, D), jnp.float32)
        for offset in range(SPAN):
            source = target - offset
            if source >= 0:
                summed = summed + jnp.dot(latents[source], dec_weight[source, offset], preferred_element_type=jnp.float32)
        recons.append(summed.astype(jnp.bfloat16))
        errors.append((0.25 * (summed - targets[target].astype(jnp.float32))).astype(jnp.bfloat16))
    grads = []
    lat_grads = []
    for source in range(LAYERS):
        per_offset = []
        lat_grad = jnp.zeros((TOK, LATENTS), jnp.float32)
        for offset in range(SPAN):
            target = source + offset
            if target < LAYERS:
                per_offset.append(jnp.dot(latents[source].T, errors[target], preferred_element_type=jnp.float32).astype(jnp.bfloat16))
                lat_grad = lat_grad + jnp.dot(errors[target], dec_weight[source, offset].T, preferred_element_type=jnp.float32)
            else:
                per_offset.append(jnp.zeros((LATENTS, D), jnp.bfloat16))
        grads.append(jnp.stack(per_offset, axis=0))
        lat_grads.append(lat_grad.astype(jnp.bfloat16))
    return jnp.stack(recons, axis=0), jnp.stack(grads, axis=0), jnp.stack(lat_grads, axis=0)
```

```python
import jax
import jax.numpy as jnp
from jax import lax
from jax.sharding import Mesh, PartitionSpec as P

BF = jnp.bfloat16
F32 = jnp.float32


def swap_cores(block):
    return lax.ppermute(block, "core", [(0, 1), (1, 0)])


def exchange_z(block, first, second):
    route = [
        (2 * z + c, 2 * (z ^ (second if c else first)) + c)
        for z in range(lax.axis_size("zh"))
        for c in range(2)
    ]
    return lax.ppermute(block, ("zh", "core"), route)


def shift_layer(block, distance):
    count = lax.axis_size(("zl", "x"))
    route = [(i, i + distance) for i in range(count) if 0 <= i + distance < count]
    return lax.ppermute(block, ("zl", "x"), route)


def per_device(residual, targets, enc_weight, enc_bias, dec_weight):
    w_encode = enc_weight[0]
    bias_row = enc_bias[0]
    decoder = dec_weight[0]
    target = targets[0].astype(F32)
    z_at = lax.axis_index("zh") * 16
    core = lax.axis_index("core")

    mine = lax.all_gather(residual[0], "zh", axis=0, tiled=True)
    mine = lax.all_gather(mine, "y", axis=0, tiled=True)
    other = swap_cores(mine)

    def encode(rows):
        pre = jnp.dot(rows, w_encode, preferred_element_type=F32) + bias_row
        return jax.nn.relu(pre).astype(BF)

    lat_mine = encode(mine)
    lat_other = encode(other)

    def decode(lat):
        return jnp.concatenate(
            [jnp.dot(lat, decoder[s], preferred_element_type=F32) for s in range(2)], axis=1
        )

    received = swap_cores(decode(lat_other).astype(BF))
    part = (decode(lat_mine) + received.astype(F32)).astype(BF)
    part = lax.all_to_all(part, "y", 0, 0, tiled=True)
    part = jnp.sum(part.reshape(4, 64, 2048).astype(F32), axis=0)
    shifted = shift_layer(part[:, 1024:].astype(BF), 1)
    part = part[:, :1024] + shifted.astype(F32)
    own = lax.dynamic_slice(part, (z_at, 0), (16, 1024)) - target
    part = lax.dynamic_update_slice(part, own, (z_at, 0))
    part = part + exchange_z(part.astype(BF), 1, 3).astype(F32)
    part = part + exchange_z(part.astype(BF), 3, 1).astype(F32)
    recon = (lax.dynamic_slice(part, (z_at, 0), (16, 1024)) + target).astype(BF)

    error = (0.25 * part).astype(BF)
    both = jnp.stack([error, shift_layer(error, -1)])
    both = jnp.broadcast_to(both, (4, 2, 64, 1024))
    mine_err = lax.all_to_all(both, "y", 0, 0, tiled=True).reshape(512, 1024)
    other_err = swap_cores(mine_err)

    def tokens(a, b):
        a0 = jnp.where(core == 0, a, b)
        a1 = jnp.where(core == 0, b, a)
        st = jnp.stack([a0, a1], axis=1)
        return st

    def split(err):
        err = err.reshape(4, 2, 64, 1024)
        return err[:, 0].reshape(256, 1024), err[:, 1].reshape(256, 1024)

    e_mine, e_other = split(mine_err), split(other_err)
    lat_grad = []
    for e in (e_mine, e_other):
        lat_grad.append(
            sum(
                lax.dot_general(e[s], decoder[s], (((1,), (1,)), ((), ())), preferred_element_type=F32)
                for s in range(2)
            )
            .astype(BF)
            .reshape(4, 4, 16, 384)
        )
    first = jnp.where(core == 0, lat_grad[0], lat_grad[1])
    second = jnp.where(core == 0, lat_grad[1], lat_grad[0])
    lat_out = jnp.stack([first, second], axis=2).transpose(1, 0, 2, 3, 4).reshape(512, 384)
    dec_grad = []
    for s in range(2):
        total = sum(
            lax.dot_general(lat, e[s], (((0,), (0,)), ((), ())), preferred_element_type=F32)
            for lat, e in ((lat_mine, e_mine), (lat_other, e_other))
        )
        dec_grad.append(total.astype(BF))
    return recon[None], jnp.stack(dec_grad)[None], lat_out[None]


def solution(mesh):
    grid = Mesh(mesh.devices.reshape(4, 4, 4, 4, 2), ("zl", "x", "zh", "y", "core"))
    layer, latent = ("zl", "x"), ("zh", "y", "core")
    return jax.shard_map(
        per_device,
        mesh=grid,
        in_specs=(
            P(layer, latent, None),
            P(layer, latent, None),
            P(layer, None, latent),
            P(layer, latent),
            P(layer, None, latent, None),
        ),
        out_specs=(
            P(layer, latent, None),
            P(layer, None, latent, None),
            P(layer, None, latent),
        ),
        check_vma=False,
    )
```

```python
import jax
import jax.numpy as jnp
from jax import lax
from jax.experimental import pallas as pl
from jax.experimental.pallas import tpu as pltpu
from jax.sharding import PartitionSpec as P

BF = jnp.bfloat16
F32 = jnp.float32


def place(z, y, rows):
    return 8 * z + 2 * y + ((rows ^ z ^ y) & 1)


ALONG_Z = [[place(z, y, r) for z in range(4)] for y in range(4) for r in range(2)]
ALONG_Y = [[place(z, y, r) for y in range(4)] for z in range(4) for r in range(2)]


def swap_cores(block):
    return lax.ppermute(block, "latent", [(i, i ^ 1) for i in range(32)])


def exchange_z(block, first, second):
    route = [
        (place(z, y, r), place(z ^ (second if r else first), y, r))
        for z in range(4)
        for y in range(4)
        for r in range(2)
    ]
    return lax.ppermute(block, "latent", route)


def shift_layer(block, distance):
    count = lax.axis_size("layer")
    route = [(i, i + distance) for i in range(count) if 0 <= i + distance < count]
    return lax.ppermute(block, "layer", route)


VMEM = pl.BlockSpec(memory_space=pltpu.VMEM)
ANYWHERE = pl.BlockSpec(memory_space=pl.ANY)
ACROSS = (((1,), (1,)), ((), ()))


def call(kernel, outs, specs, out_specs, flops, scratch=()):
    return pl.pallas_call(
        kernel,
        out_shape=outs,
        in_specs=specs,
        out_specs=out_specs,
        scratch_shapes=scratch,
        compiler_params=pltpu.CompilerParams(vmem_limit_bytes=32 * 1024 * 1024),
        cost_estimate=pl.CostEstimate(flops=flops, bytes_accessed=2_000_000, transcendentals=0),
    )


def copies_kernel(own_ref, next_ref, out_ref):
    for y in range(4):
        out_ref[y, 0] = own_ref[...]
        out_ref[y, 1] = next_ref[...]


def copies(own, after):
    out = jax.ShapeDtypeStruct((4, 2, 64, 1024), BF)
    return call(copies_kernel, out, [VMEM] * 2, VMEM, 1)(own, after)


def rows_of(err_ref, s):
    return err_ref[:, s].reshape(256, 1024)


def latent_rows(err_ref, dec_ref):
    total = lax.dot_general(rows_of(err_ref, 0), dec_ref[0], ACROSS, preferred_element_type=F32)
    total += lax.dot_general(rows_of(err_ref, 1), dec_ref[1], ACROSS, preferred_element_type=F32)
    return total.astype(BF)


def first_kernel(err_ref, lat_ref, dec_ref, parts_ref, held_ref):
    for s in range(2):
        parts_ref[s] = jnp.dot(lat_ref[...], rows_of(err_ref, s), preferred_element_type=F32)
    held_ref[...] = latent_rows(err_ref, dec_ref)


def first_gradients(err, lat_t, decoder):
    outs = (jax.ShapeDtypeStruct((2, 384, 1024), F32), jax.ShapeDtypeStruct((256, 384), BF))
    return call(first_kernel, outs, [VMEM] * 3, (VMEM, VMEM), 805_306_368)(err, lat_t, decoder)


def last_kernel(set_ref, err_ref, lat_ref, dec_ref, parts_ref, held_ref, dec_out, lat_out, dec_buf, lat_buf, sems):
    even = set_ref[0] * 16
    sends = [pltpu.make_async_copy(dec_buf.at[s], dec_out.at[s], sems.at[s]) for s in range(2)]
    sends.append(pltpu.make_async_copy(lat_buf, lat_out, sems.at[2]))
    for s in range(2):
        total = parts_ref[s] + jnp.dot(lat_ref[...], rows_of(err_ref, s), preferred_element_type=F32)
        dec_buf[s] = total.astype(BF)
        sends[s].start()
    total = latent_rows(err_ref, dec_ref)
    for y in range(4):
        for z in range(4):
            here = y * 64 + z * 16
            there = z * 128 + y * 32
            at = even if (y ^ z) & 1 == 0 else 16 - even
            away = 16 - at
            lat_buf[pl.ds(pl.multiple_of(there + at, 16), 16), :] = held_ref[here : here + 16, :]
            lat_buf[pl.ds(pl.multiple_of(there + away, 16), 16), :] = total[here : here + 16, :]
    sends[2].start()
    for send in sends:
        send.wait()


def last_gradients(row_set, err, lat_t, decoder, parts, held):
    outs = (jax.ShapeDtypeStruct((2, 384, 1024), BF), jax.ShapeDtypeStruct((512, 384), BF))
    specs = [pl.BlockSpec(memory_space=pltpu.SMEM)] + [VMEM] * 5
    scratch = [pltpu.VMEM((2, 384, 1024), BF), pltpu.VMEM((512, 384), BF), pltpu.SemaphoreType.DMA((3,))]
    return call(last_kernel, outs, specs, (ANYWHERE, ANYWHERE), 805_306_368, scratch)(
        row_set.reshape(1), err, lat_t, decoder, parts, held
    )


def per_device(residual, targets, enc_weight, enc_bias, dec_weight):
    w_encode = enc_weight[0]
    bias_row = enc_bias[0]
    decoder = dec_weight[0]
    target = targets[0].astype(F32)
    latent = lax.axis_index("latent")
    z_at = (latent // 8) * 16
    row_set = (latent ^ (latent // 2) ^ (latent // 8)) & 1

    mine = lax.all_gather(residual[0], "latent", axis=0, tiled=True, axis_index_groups=ALONG_Z)
    mine = lax.all_gather(mine, "latent", axis=0, tiled=True, axis_index_groups=ALONG_Y)
    other = swap_cores(mine)

    def encode(rows):
        pre = jnp.dot(rows, w_encode, preferred_element_type=F32) + bias_row
        return jax.nn.relu(pre).astype(BF)

    lat_mine = encode(mine)
    lat_other = encode(other)

    def decode(lat):
        return jnp.concatenate(
            [jnp.dot(lat, decoder[s], preferred_element_type=F32) for s in range(2)], axis=1
        )

    received = swap_cores(decode(lat_other).astype(BF))
    part = (decode(lat_mine) + received.astype(F32)).astype(BF)
    part = lax.all_to_all(part, "latent", 0, 0, tiled=True, axis_index_groups=ALONG_Y)
    part = jnp.sum(part.reshape(4, 64, 2048).astype(F32), axis=0)
    shifted = shift_layer(part[:, 1024:].astype(BF), 1)
    part = part[:, :1024] + shifted.astype(F32)
    own = lax.dynamic_slice(part, (z_at, 0), (16, 1024)) - target
    part = lax.dynamic_update_slice(part, own, (z_at, 0))
    part = part + exchange_z(part.astype(BF), 1, 3).astype(F32)
    part = part + exchange_z(part.astype(BF), 3, 1).astype(F32)
    recon = (lax.dynamic_slice(part, (z_at, 0), (16, 1024)) + target).astype(BF)

    error = (0.25 * part).astype(BF)
    after, recon = lax.optimization_barrier((shift_layer(error, -1), recon))
    both = copies(error, after)
    mine_err = lax.all_to_all(both, "latent", 0, 0, tiled=True, axis_index_groups=ALONG_Y)
    other_err = swap_cores(mine_err)
    parts, held = first_gradients(mine_err, lat_mine.T, decoder)
    dec_grad, lat_grad = last_gradients(row_set, other_err, lat_other.T, decoder, parts, held)
    return recon[None], dec_grad[None], lat_grad[None]


def solution(mesh):
    return jax.shard_map(
        per_device,
        mesh=mesh,
        in_specs=(
            P("layer", "latent", None),
            P("layer", "latent", None),
            P("layer", None, "latent"),
            P("layer", "latent"),
            P("layer", None, "latent", None),
        ),
        out_specs=(
            P("layer", "latent", None),
            P("layer", None, "latent", None),
            P("layer", None, "latent"),
        ),
        check_vma=False,
    )
```

```python
import jax
import jax.numpy as jnp
from jax import lax
from jax.experimental import pallas as pl
from jax.experimental.pallas import tpu as pltpu
from jax.sharding import PartitionSpec as P

BF = jnp.bfloat16
F32 = jnp.float32


def place(z, y, rows):
    return 8 * z + 2 * y + ((rows ^ z ^ y) & 1)


ALONG_Z = [[place(z, y, r) for z in range(4)] for y in range(4) for r in range(2)]
ALONG_Y = [[place(z, y, r) for y in range(4)] for z in range(4) for r in range(2)]


def swap_cores(block):
    return lax.ppermute(block, "latent", [(i, i ^ 1) for i in range(32)])


def exchange_z(block, first, second):
    route = [
        (place(z, y, r), place(z ^ (second if r else first), y, r))
        for z in range(4)
        for y in range(4)
        for r in range(2)
    ]
    return lax.ppermute(block, "latent", route)


def shift_layer(block, distance):
    count = lax.axis_size("layer")
    route = [(i, i + distance) for i in range(count) if 0 <= i + distance < count]
    return lax.ppermute(block, "layer", route)


VMEM = pl.BlockSpec(memory_space=pltpu.VMEM)
ANYWHERE = pl.BlockSpec(memory_space=pl.ANY)
ACROSS = (((1,), (1,)), ((), ()))


def call(kernel, outs, specs, out_specs, flops, scratch=()):
    return pl.pallas_call(
        kernel,
        out_shape=outs,
        in_specs=specs,
        out_specs=out_specs,
        scratch_shapes=scratch,
        compiler_params=pltpu.CompilerParams(vmem_limit_bytes=32 * 1024 * 1024),
        cost_estimate=pl.CostEstimate(flops=flops, bytes_accessed=2_000_000, transcendentals=0),
    )


def pack_kernel(enc_ref, bias_ref, dec_ref, out_ref, bias_buf, sems):
    loads = [
        pltpu.make_async_copy(dec_ref.at[0], out_ref.at[0:384], sems.at[0]),
        pltpu.make_async_copy(dec_ref.at[1], out_ref.at[384:768], sems.at[1]),
        pltpu.make_async_copy(enc_ref.at[0:512], out_ref.at[768:1280, 0:384], sems.at[2]),
        pltpu.make_async_copy(enc_ref.at[512:1024], out_ref.at[768:1280, 384:768], sems.at[3]),
    ]
    bias_load = pltpu.make_async_copy(bias_ref, bias_buf, sems.at[4])
    bias_load.start()
    for load in loads:
        load.start()
    bias_load.wait()
    rest = jnp.broadcast_to(bias_buf[...], (16, 384))
    row = lax.broadcasted_iota(jnp.int32, (16, 384), 0)
    rows = jnp.zeros((16, 384), F32)
    for i in range(3):
        piece = rest.astype(BF).astype(F32)
        rows = jnp.where(row == i, piece, rows)
        rest = rest - piece
    out_ref[1280:1296, 0:384] = rows.astype(BF)
    for load in loads:
        load.wait()


def pack(encoder, bias, decoder):
    out = jax.ShapeDtypeStruct((1296, 1024), BF)
    scratch = [pltpu.VMEM((1, 384), F32), pltpu.SemaphoreType.DMA((5,))]
    encoder, bias, decoder = (pltpu.with_memory_space_constraint(a, pltpu.HBM) for a in (encoder, bias, decoder))
    return call(pack_kernel, out, [ANYWHERE] * 3, VMEM, 1, scratch)(
        encoder, bias, decoder
    )


def forward_kernel(rows_ref, own_ref, sib_ref, part_ref, lat_ref, other_ref):
    def dot(a, b):
        return jnp.dot(a, b, preferred_element_type=F32)

    lats = []
    for from_ref, to_ref in ((own_ref, lat_ref), (sib_ref, other_ref)):
        pieces = from_ref[1280:1296, 0:384].astype(F32)
        lat = dot(rows_ref[:, 0:512], from_ref[768:1280, 0:384])
        lat += dot(rows_ref[:, 512:1024], from_ref[768:1280, 384:768])
        lat += pieces[0:1] + pieces[1:2] + pieces[2:3]
        lats.append(jnp.maximum(lat, 0.0).astype(BF))
        to_ref[...] = lats[-1]
    for s in range(2):
        decoder = slice(384 * s, 384 * (s + 1))
        total = dot(lats[0], own_ref[decoder, :]) + dot(lats[1], sib_ref[decoder, :])
        part_ref[:, :, 1024 * s : 1024 * (s + 1)] = total.astype(BF).reshape(4, 64, 1024)


def forward(rows, own, sibling):
    outs = (
        jax.ShapeDtypeStruct((4, 64, 2048), BF),
        jax.ShapeDtypeStruct((256, 384), BF),
        jax.ShapeDtypeStruct((256, 384), BF),
    )
    return call(forward_kernel, outs, [VMEM] * 3, (VMEM,) * 3, 1_207_959_552)(rows, own, sibling)


def copies_kernel(own_ref, next_ref, out_ref):
    for y in range(4):
        out_ref[y, 0] = own_ref[...]
        out_ref[y, 1] = next_ref[...]


def copies(own, after):
    out = jax.ShapeDtypeStruct((4, 2, 64, 1024), BF)
    return call(copies_kernel, out, [VMEM] * 2, VMEM, 1)(own, after)


def rows_of(err_ref, s):
    return err_ref[:, s].reshape(256, 1024)


def latent_rows(err_ref, dec_ref):
    total = lax.dot_general(rows_of(err_ref, 0), dec_ref[0], ACROSS, preferred_element_type=F32)
    total += lax.dot_general(rows_of(err_ref, 1), dec_ref[1], ACROSS, preferred_element_type=F32)
    return total.astype(BF)


def first_kernel(err_ref, lat_ref, dec_ref, parts_ref, held_ref):
    for s in range(2):
        parts_ref[s] = jnp.dot(lat_ref[...], rows_of(err_ref, s), preferred_element_type=F32)
    held_ref[...] = latent_rows(err_ref, dec_ref)


def first_gradients(err, lat_t, decoder):
    outs = (jax.ShapeDtypeStruct((2, 384, 1024), F32), jax.ShapeDtypeStruct((256, 384), BF))
    return call(first_kernel, outs, [VMEM] * 3, (VMEM, VMEM), 805_306_368)(err, lat_t, decoder)


def last_kernel(set_ref, err_ref, lat_ref, dec_ref, parts_ref, held_ref, dec_out, lat_out, dec_buf, lat_buf, sems):
    even = set_ref[0] * 16
    sends = [pltpu.make_async_copy(dec_buf.at[s], dec_out.at[s], sems.at[s]) for s in range(2)]
    sends.append(pltpu.make_async_copy(lat_buf, lat_out, sems.at[2]))
    for s in range(2):
        total = parts_ref[s] + jnp.dot(lat_ref[...], rows_of(err_ref, s), preferred_element_type=F32)
        dec_buf[s] = total.astype(BF)
        sends[s].start()
    total = latent_rows(err_ref, dec_ref)
    for y in range(4):
        for z in range(4):
            here = y * 64 + z * 16
            there = z * 128 + y * 32
            at = even if (y ^ z) & 1 == 0 else 16 - even
            away = 16 - at
            lat_buf[pl.ds(pl.multiple_of(there + at, 16), 16), :] = held_ref[here : here + 16, :]
            lat_buf[pl.ds(pl.multiple_of(there + away, 16), 16), :] = total[here : here + 16, :]
    sends[2].start()
    for send in sends:
        send.wait()


def last_gradients(row_set, err, lat_t, decoder, parts, held):
    outs = (jax.ShapeDtypeStruct((2, 384, 1024), BF), jax.ShapeDtypeStruct((512, 384), BF))
    specs = [pl.BlockSpec(memory_space=pltpu.SMEM)] + [VMEM] * 5
    scratch = [pltpu.VMEM((2, 384, 1024), BF), pltpu.VMEM((512, 384), BF), pltpu.SemaphoreType.DMA((3,))]
    return call(last_kernel, outs, specs, (ANYWHERE, ANYWHERE), 805_306_368, scratch)(
        row_set.reshape(1), err, lat_t, decoder, parts, held
    )


def per_device(residual, targets, enc_weight, enc_bias, dec_weight):
    w_encode = enc_weight[0]
    decoder = dec_weight[0]
    target = targets[0].astype(F32)
    latent = lax.axis_index("latent")
    z_at = (latent // 8) * 16
    row_set = (latent ^ (latent // 2) ^ (latent // 8)) & 1

    packed = pack(w_encode, enc_bias, decoder)
    sibling = swap_cores(packed)

    mine = lax.all_gather(residual[0], "latent", axis=0, tiled=True, axis_index_groups=ALONG_Z)
    mine, sibling = lax.optimization_barrier((mine, sibling))
    mine = lax.all_gather(mine, "latent", axis=0, tiled=True, axis_index_groups=ALONG_Y)
    part, lat_mine, lat_sibling = forward(mine, packed, sibling)
    lat_other = swap_cores(lat_sibling)
    part = lax.all_to_all(part, "latent", 0, 0, tiled=True, axis_index_groups=ALONG_Y)
    part = jnp.sum(part.astype(F32), axis=0)
    shifted = shift_layer(part[:, 1024:].astype(BF), 1)
    shifted, lat_t, other_t = lax.optimization_barrier((shifted, lat_mine.T, lat_other.T))
    part = part[:, :1024] + shifted.astype(F32)
    own = lax.dynamic_slice(part, (z_at, 0), (16, 1024)) - target
    part = lax.dynamic_update_slice(part, own, (z_at, 0))
    part = part + exchange_z(part.astype(BF), 1, 3).astype(F32)
    part = part + exchange_z(part.astype(BF), 3, 1).astype(F32)
    recon = (lax.dynamic_slice(part, (z_at, 0), (16, 1024)) + target).astype(BF)

    error = (0.25 * part).astype(BF)
    after, recon = lax.optimization_barrier((shift_layer(error, -1), recon))
    both = copies(error, after)
    mine_err = lax.all_to_all(both, "latent", 0, 0, tiled=True, axis_index_groups=ALONG_Y)
    other_err = swap_cores(mine_err)
    parts, held = first_gradients(mine_err, lat_t, decoder)
    dec_grad, lat_grad = last_gradients(row_set, other_err, other_t, decoder, parts, held)
    return recon[None], dec_grad[None], lat_grad[None]


def solution(mesh):
    return jax.shard_map(
        per_device,
        mesh=mesh,
        in_specs=(
            P("layer", "latent", None),
            P("layer", "latent", None),
            P("layer", None, "latent"),
            P("layer", "latent"),
            P("layer", None, "latent", None),
        ),
        out_specs=(
            P("layer", "latent", None),
            P("layer", None, "latent", None),
            P("layer", None, "latent"),
        ),
        check_vma=False,
    )
```

```python
import jax
import jax.numpy as jnp
from jax import lax
from jax.experimental import pallas as pl
from jax.experimental.pallas import tpu as pltpu
from jax.sharding import PartitionSpec as P

BF = jnp.bfloat16
F32 = jnp.float32


def place(z, y, rows):
    return 8 * z + 2 * y + ((rows ^ z ^ y) & 1)


ALONG_Z = [[place(z, y, r) for z in range(4)] for y in range(4) for r in range(2)]
ALONG_Y = [[place(z, y, r) for y in range(4)] for z in range(4) for r in range(2)]


def swap_cores(block):
    return lax.ppermute(block, "latent", [(i, i ^ 1) for i in range(32)])


def exchange_z(block, first, second):
    route = [
        (place(z, y, r), place(z ^ (second if r else first), y, r))
        for z in range(4)
        for y in range(4)
        for r in range(2)
    ]
    return lax.ppermute(block, "latent", route)


def shift_layer(block, distance):
    count = lax.axis_size("layer")
    route = [(i, i + distance) for i in range(count) if 0 <= i + distance < count]
    return lax.ppermute(block, "layer", route)


VMEM = pl.BlockSpec(memory_space=pltpu.VMEM)
ANYWHERE = pl.BlockSpec(memory_space=pl.ANY)
ACROSS = (((1,), (1,)), ((), ()))


def call(kernel, outs, specs, out_specs, flops, scratch=()):
    return pl.pallas_call(
        kernel,
        out_shape=outs,
        in_specs=specs,
        out_specs=out_specs,
        scratch_shapes=scratch,
        compiler_params=pltpu.CompilerParams(vmem_limit_bytes=32 * 1024 * 1024),
        cost_estimate=pl.CostEstimate(flops=flops, bytes_accessed=2_000_000, transcendentals=0),
    )


def pack_kernel(enc_ref, bias_ref, dec_ref, out_ref, bias_buf, sems):
    loads = [
        pltpu.make_async_copy(dec_ref.at[0], out_ref.at[0:384], sems.at[0]),
        pltpu.make_async_copy(dec_ref.at[1], out_ref.at[384:768], sems.at[1]),
        pltpu.make_async_copy(enc_ref.at[0:512], out_ref.at[768:1280, 0:384], sems.at[2]),
        pltpu.make_async_copy(enc_ref.at[512:1024], out_ref.at[768:1280, 384:768], sems.at[3]),
    ]
    bias_load = pltpu.make_async_copy(bias_ref, bias_buf, sems.at[4])
    bias_load.start()
    for load in loads:
        load.start()
    bias_load.wait()
    rest = jnp.broadcast_to(bias_buf[...], (16, 384))
    row = lax.broadcasted_iota(jnp.int32, (16, 384), 0)
    rows = jnp.zeros((16, 384), F32)
    for i in range(3):
        piece = rest.astype(BF).astype(F32)
        rows = jnp.where(row == i, piece, rows)
        rest = rest - piece
    out_ref[1280:1296, 0:384] = rows.astype(BF)
    for load in loads:
        load.wait()


def pack(encoder, bias, decoder):
    out = jax.ShapeDtypeStruct((1296, 1024), BF)
    scratch = [pltpu.VMEM((1, 384), F32), pltpu.SemaphoreType.DMA((5,))]
    encoder, bias, decoder = (pltpu.with_memory_space_constraint(a, pltpu.HBM) for a in (encoder, bias, decoder))
    return call(pack_kernel, out, [ANYWHERE] * 3, VMEM, 1, scratch)(
        encoder, bias, decoder
    )


def forward_kernel(rows_ref, own_ref, sib_ref, part_ref, lat_ref, other_ref):
    def dot(a, b):
        return jnp.dot(a, b, preferred_element_type=F32)

    lats = []
    for from_ref, to_ref in ((own_ref, lat_ref), (sib_ref, other_ref)):
        pieces = from_ref[1280:1296, 0:384].astype(F32)
        lat = dot(rows_ref[:, 0:512], from_ref[768:1280, 0:384])
        lat += dot(rows_ref[:, 512:1024], from_ref[768:1280, 384:768])
        lat += pieces[0:1] + pieces[1:2] + pieces[2:3]
        lats.append(jnp.maximum(lat, 0.0).astype(BF))
        to_ref[...] = lats[-1]
    for s in range(2):
        decoder = slice(384 * s, 384 * (s + 1))
        total = dot(lats[0], own_ref[decoder, :]) + dot(lats[1], sib_ref[decoder, :])
        part_ref[:, :, 1024 * s : 1024 * (s + 1)] = total.astype(BF).reshape(4, 64, 1024)


def forward(rows, own, sibling):
    outs = (
        jax.ShapeDtypeStruct((4, 64, 2048), BF),
        jax.ShapeDtypeStruct((256, 384), BF),
        jax.ShapeDtypeStruct((256, 384), BF),
    )
    return call(forward_kernel, outs, [VMEM] * 3, (VMEM,) * 3, 1_207_959_552)(rows, own, sibling)


def copies_kernel(own_ref, next_ref, out_ref):
    for y in range(4):
        out_ref[y, 0] = own_ref[...]
        out_ref[y, 1] = next_ref[...]


def copies(own, after):
    out = jax.ShapeDtypeStruct((4, 2, 64, 1024), BF)
    return call(copies_kernel, out, [VMEM] * 2, VMEM, 1)(own, after)


def rows_of(err_ref, s):
    return err_ref[:, s].reshape(256, 1024)


def latent_rows(err_ref, dec_ref):
    total = lax.dot_general(rows_of(err_ref, 0), dec_ref[0], ACROSS, preferred_element_type=F32)
    total += lax.dot_general(rows_of(err_ref, 1), dec_ref[1], ACROSS, preferred_element_type=F32)
    return total.astype(BF)


def first_kernel(err_ref, lat_ref, dec_ref, parts_ref, held_ref):
    for s in range(2):
        parts_ref[s] = jnp.dot(lat_ref[...], rows_of(err_ref, s), preferred_element_type=F32)
    held_ref[...] = latent_rows(err_ref, dec_ref)


def first_gradients(err, lat_t, decoder):
    outs = (jax.ShapeDtypeStruct((2, 384, 1024), F32), jax.ShapeDtypeStruct((256, 384), BF))
    return call(first_kernel, outs, [VMEM] * 3, (VMEM, VMEM), 805_306_368)(err, lat_t, decoder)


def last_kernel(set_ref, err_ref, lat_ref, dec_ref, parts_ref, held_ref, dec_out, lat_out, dec_buf, lat_buf, sems):
    even = set_ref[0] * 16
    sends = [pltpu.make_async_copy(dec_buf.at[s], dec_out.at[s], sems.at[s]) for s in range(2)]
    sends.append(pltpu.make_async_copy(lat_buf, lat_out, sems.at[2]))
    for s in range(2):
        total = parts_ref[s] + jnp.dot(lat_ref[...], rows_of(err_ref, s), preferred_element_type=F32)
        dec_buf[s] = total.astype(BF)
        sends[s].start()
    total = latent_rows(err_ref, dec_ref)
    for y in range(4):
        for z in range(4):
            here = y * 64 + z * 16
            there = z * 128 + y * 32
            at = even if (y ^ z) & 1 == 0 else 16 - even
            away = 16 - at
            lat_buf[pl.ds(pl.multiple_of(there + at, 16), 16), :] = held_ref[here : here + 16, :]
            lat_buf[pl.ds(pl.multiple_of(there + away, 16), 16), :] = total[here : here + 16, :]
    sends[2].start()
    for send in sends:
        send.wait()


def last_gradients(row_set, err, lat_t, decoder, parts, held):
    outs = (jax.ShapeDtypeStruct((2, 384, 1024), BF), jax.ShapeDtypeStruct((512, 384), BF))
    specs = [pl.BlockSpec(memory_space=pltpu.SMEM)] + [VMEM] * 5
    scratch = [pltpu.VMEM((2, 384, 1024), BF), pltpu.VMEM((512, 384), BF), pltpu.SemaphoreType.DMA((3,))]
    return call(last_kernel, outs, specs, (ANYWHERE, ANYWHERE), 805_306_368, scratch)(
        row_set.reshape(1), err, lat_t, decoder, parts, held
    )


def per_device(residual, targets, enc_weight, enc_bias, dec_weight):
    w_encode = enc_weight[0]
    decoder = dec_weight[0]
    target = targets[0].astype(F32)
    latent = lax.axis_index("latent")
    z_at = (latent // 8) * 16
    row_set = (latent ^ (latent // 2) ^ (latent // 8)) & 1

    packed = pack(w_encode, enc_bias, decoder)
    sibling = swap_cores(packed)

    mine = lax.all_gather(residual[0], "latent", axis=0, tiled=True, axis_index_groups=ALONG_Z)
    mine, sibling = lax.optimization_barrier((mine, sibling))
    mine = lax.all_gather(mine, "latent", axis=0, tiled=True, axis_index_groups=ALONG_Y)
    part, lat_mine, lat_sibling = forward(mine, packed, sibling)
    part = lax.all_to_all(part, "latent", 0, 0, tiled=True, axis_index_groups=ALONG_Y)
    part = jnp.sum(part.astype(F32), axis=0)
    shifted = shift_layer(part[:, 1024:].astype(BF), 1)
    shifted, lat_t, lat_sibling = lax.optimization_barrier((shifted, lat_mine.T, lat_sibling))
    part = part[:, :1024] + shifted.astype(F32)
    own = lax.dynamic_slice(part, (z_at, 0), (16, 1024)) - target
    part = lax.dynamic_update_slice(part, own, (z_at, 0))
    halves = [swap_cores(lat_sibling[:128]), swap_cores(lat_sibling[128:])]
    met, *halves = lax.optimization_barrier((exchange_z(part.astype(BF), 1, 3), *halves))
    other_t = jnp.concatenate(halves).T
    part = part + met.astype(F32)
    part = part + exchange_z(part.astype(BF), 3, 1).astype(F32)
    recon = (lax.dynamic_slice(part, (z_at, 0), (16, 1024)) + target).astype(BF)

    error = (0.25 * part).astype(BF)
    after, recon, other_t = lax.optimization_barrier((shift_layer(error, -1), recon, other_t))
    both = copies(error, after)
    mine_err = lax.all_to_all(both, "latent", 0, 0, tiled=True, axis_index_groups=ALONG_Y)
    other_err = swap_cores(mine_err)
    parts, held = first_gradients(mine_err, lat_t, decoder)
    dec_grad, lat_grad = last_gradients(row_set, other_err, other_t, decoder, parts, held)
    return recon[None], dec_grad[None], lat_grad[None]


def solution(mesh):
    return jax.shard_map(
        per_device,
        mesh=mesh,
        in_specs=(
            P("layer", "latent", None),
            P("layer", "latent", None),
            P("layer", None, "latent"),
            P("layer", "latent"),
            P("layer", None, "latent", None),
        ),
        out_specs=(
            P("layer", "latent", None),
            P("layer", None, "latent", None),
            P("layer", None, "latent"),
        ),
        check_vma=False,
    )
```

```python
import jax
import jax.numpy as jnp
from jax import lax
from jax.experimental import pallas as pl
from jax.experimental.pallas import tpu as pltpu
from jax.sharding import PartitionSpec as P

BF = jnp.bfloat16
F32 = jnp.float32


def place(z, y, rows):
    return 8 * z + 2 * y + ((rows ^ z ^ y) & 1)


ALONG_Z = [[place(z, y, r) for z in range(4)] for y in range(4) for r in range(2)]
ALONG_Y = [[place(z, y, r) for y in range(4)] for z in range(4) for r in range(2)]


def swap_cores(block):
    return lax.ppermute(block, "latent", [(i, i ^ 1) for i in range(32)])


def exchange_z(block, first, second):
    route = [
        (place(z, y, r), place(z ^ (second if r else first), y, r))
        for z in range(4)
        for y in range(4)
        for r in range(2)
    ]
    return lax.ppermute(block, "latent", route)


def shift_layer(block, distance):
    count = lax.axis_size("layer")
    route = [(i, i + distance) for i in range(count) if 0 <= i + distance < count]
    return lax.ppermute(block, "layer", route)


VMEM = pl.BlockSpec(memory_space=pltpu.VMEM)
ANYWHERE = pl.BlockSpec(memory_space=pl.ANY)
ACROSS = (((1,), (1,)), ((), ()))


def call(kernel, outs, specs, out_specs, flops, scratch=()):
    return pl.pallas_call(
        kernel,
        out_shape=outs,
        in_specs=specs,
        out_specs=out_specs,
        scratch_shapes=scratch,
        compiler_params=pltpu.CompilerParams(vmem_limit_bytes=32 * 1024 * 1024),
        cost_estimate=pl.CostEstimate(flops=flops, bytes_accessed=2_000_000, transcendentals=0),
    )


def pack_kernel(enc_ref, bias_ref, dec_ref, out_ref, bias_buf, sems):
    pairs = [(dec_ref.at[i, pl.ds(j, 128)], out_ref.at[pl.ds(384 * i + j, 128)]) for i in range(2) for j in (0, 128, 256)]
    pairs += [
        (enc_ref.at[pl.ds(512 * i + j, 256)], out_ref.at[pl.ds(768 + j, 256), pl.ds(384 * i, 384)])
        for i in range(2)
        for j in (0, 256)
    ]
    loads = [pltpu.make_async_copy(pair[0], pair[1], sems.at[i]) for i, pair in enumerate(pairs)]
    bias_load = pltpu.make_async_copy(bias_ref, bias_buf, sems.at[10])
    bias_load.start()
    for load in loads:
        load.start()
    bias_load.wait()
    rest = jnp.broadcast_to(bias_buf[...], (16, 384))
    row = lax.broadcasted_iota(jnp.int32, (16, 384), 0)
    rows = jnp.zeros((16, 384), F32)
    for i in range(3):
        piece = rest.astype(BF).astype(F32)
        rows = jnp.where(row == i, piece, rows)
        rest = rest - piece
    out_ref[1280:1296, 0:384] = rows.astype(BF)
    for load in loads:
        load.wait()


def pack(encoder, bias, decoder):
    out = jax.ShapeDtypeStruct((1296, 1024), BF)
    scratch = [pltpu.VMEM((1, 384), F32), pltpu.SemaphoreType.DMA((11,))]
    encoder, bias, decoder = (pltpu.with_memory_space_constraint(a, pltpu.HBM) for a in (encoder, bias, decoder))
    return call(pack_kernel, out, [ANYWHERE] * 3, VMEM, 1, scratch)(
        encoder, bias, decoder
    )


def forward_kernel(rows_ref, own_ref, sib_ref, part_ref, lat_ref, other_ref):
    def dot(a, b):
        return jnp.dot(a, b, preferred_element_type=F32)

    lats = []
    for from_ref, to_ref in ((own_ref, lat_ref), (sib_ref, other_ref)):
        pieces = from_ref[1280:1296, 0:384].astype(F32)
        lat = dot(rows_ref[:, 0:512], from_ref[768:1280, 0:384])
        lat += dot(rows_ref[:, 512:1024], from_ref[768:1280, 384:768])
        lat += pieces[0:1] + pieces[1:2] + pieces[2:3]
        lats.append(jnp.maximum(lat, 0.0).astype(BF))
        to_ref[...] = lats[-1]
    for s in range(2):
        decoder = slice(384 * s, 384 * (s + 1))
        total = dot(lats[0], own_ref[decoder, :]) + dot(lats[1], sib_ref[decoder, :])
        part_ref[:, :, 1024 * s : 1024 * (s + 1)] = total.astype(BF).reshape(4, 64, 1024)


def forward(rows, own, sibling):
    outs = (
        jax.ShapeDtypeStruct((4, 64, 2048), BF),
        jax.ShapeDtypeStruct((256, 384), BF),
        jax.ShapeDtypeStruct((256, 384), BF),
    )
    return call(forward_kernel, outs, [VMEM] * 3, (VMEM,) * 3, 1_207_959_552)(rows, own, sibling)


def copies_kernel(own_ref, next_ref, out_ref):
    for y in range(4):
        out_ref[y, 0] = own_ref[...]
        out_ref[y, 1] = next_ref[...]


def copies(own, after):
    out = jax.ShapeDtypeStruct((4, 2, 64, 1024), BF)
    return call(copies_kernel, out, [VMEM] * 2, VMEM, 1)(own, after)


def rows_of(err_ref, s):
    return err_ref[:, s].reshape(256, 1024)


def latent_rows(err_ref, dec_ref):
    total = lax.dot_general(rows_of(err_ref, 0), dec_ref[0], ACROSS, preferred_element_type=F32)
    total += lax.dot_general(rows_of(err_ref, 1), dec_ref[1], ACROSS, preferred_element_type=F32)
    return total.astype(BF)


def first_kernel(err_ref, lat_ref, dec_ref, parts_ref, held_ref):
    for s in range(2):
        parts_ref[s] = jnp.dot(lat_ref[...], rows_of(err_ref, s), preferred_element_type=F32)
    held_ref[...] = latent_rows(err_ref, dec_ref)


def first_gradients(err, lat_t, decoder):
    outs = (jax.ShapeDtypeStruct((2, 384, 1024), F32), jax.ShapeDtypeStruct((256, 384), BF))
    return call(first_kernel, outs, [VMEM] * 3, (VMEM, VMEM), 805_306_368)(err, lat_t, decoder)


def last_kernel(set_ref, err_ref, lat_ref, dec_ref, parts_ref, held_ref, dec_out, lat_out, dec_buf, lat_buf, sems):
    even = set_ref[0] * 16
    sends = [
        pltpu.make_async_copy(
            dec_buf.at[s, pl.ds(128 * i, 128)], dec_out.at[s, pl.ds(128 * i, 128)], sems.at[3 * s + i]
        )
        for s in range(2)
        for i in range(3)
    ]
    sends += [
        pltpu.make_async_copy(lat_buf.at[pl.ds(256 * i, 256)], lat_out.at[pl.ds(256 * i, 256)], sems.at[6 + i])
        for i in range(2)
    ]
    for s in range(2):
        total = parts_ref[s] + jnp.dot(lat_ref[...], rows_of(err_ref, s), preferred_element_type=F32)
        dec_buf[s] = total.astype(BF)
        for i in range(3):
            sends[3 * s + i].start()
    total = latent_rows(err_ref, dec_ref)
    for z in range(4):
        for y in range(4):
            here = y * 64 + z * 16
            there = z * 128 + y * 32
            at = even if (y ^ z) & 1 == 0 else 16 - even
            away = 16 - at
            lat_buf[pl.ds(pl.multiple_of(there + at, 16), 16), :] = held_ref[here : here + 16, :]
            lat_buf[pl.ds(pl.multiple_of(there + away, 16), 16), :] = total[here : here + 16, :]
        if z % 2:
            sends[6 + z // 2].start()
    for send in sends:
        send.wait()


def last_gradients(row_set, err, lat_t, decoder, parts, held):
    outs = (jax.ShapeDtypeStruct((2, 384, 1024), BF), jax.ShapeDtypeStruct((512, 384), BF))
    specs = [pl.BlockSpec(memory_space=pltpu.SMEM)] + [VMEM] * 5
    scratch = [pltpu.VMEM((2, 384, 1024), BF), pltpu.VMEM((512, 384), BF), pltpu.SemaphoreType.DMA((8,))]
    return call(last_kernel, outs, specs, (ANYWHERE, ANYWHERE), 805_306_368, scratch)(
        row_set.reshape(1), err, lat_t, decoder, parts, held
    )


def per_device(residual, targets, enc_weight, enc_bias, dec_weight):
    w_encode = enc_weight[0]
    decoder = dec_weight[0]
    target = targets[0].astype(F32)
    latent = lax.axis_index("latent")
    z_at = (latent // 8) * 16
    row_set = (latent ^ (latent // 2) ^ (latent // 8)) & 1

    packed = pack(w_encode, enc_bias, decoder)
    sibling = swap_cores(packed)

    mine = lax.all_gather(residual[0], "latent", axis=0, tiled=True, axis_index_groups=ALONG_Z)
    mine, sibling = lax.optimization_barrier((mine, sibling))
    mine = lax.all_gather(mine, "latent", axis=0, tiled=True, axis_index_groups=ALONG_Y)
    part, lat_mine, lat_sibling = forward(mine, packed, sibling)
    part = lax.all_to_all(part, "latent", 0, 0, tiled=True, axis_index_groups=ALONG_Y)
    part = jnp.sum(part.astype(F32), axis=0)
    shifted = shift_layer(part[:, 1024:].astype(BF), 1)
    shifted, lat_t, lat_sibling = lax.optimization_barrier((shifted, lat_mine.T, lat_sibling))
    part = part[:, :1024] + shifted.astype(F32)
    own = lax.dynamic_slice(part, (z_at, 0), (16, 1024)) - target
    part = lax.dynamic_update_slice(part, own, (z_at, 0))
    halves = [swap_cores(lat_sibling[:128]), swap_cores(lat_sibling[128:])]
    met, *halves = lax.optimization_barrier((exchange_z(part.astype(BF), 1, 3), *halves))
    other_t = jnp.concatenate(halves).T
    part = part + met.astype(F32)
    part = part + exchange_z(part.astype(BF), 3, 1).astype(F32)
    recon = (lax.dynamic_slice(part, (z_at, 0), (16, 1024)) + target).astype(BF)

    error = (0.25 * part).astype(BF)
    after, recon, other_t = lax.optimization_barrier((shift_layer(error, -1), recon, other_t))
    both = copies(error, after)
    mine_err = lax.all_to_all(both, "latent", 0, 0, tiled=True, axis_index_groups=ALONG_Y)
    other_err = swap_cores(mine_err)
    parts, held = first_gradients(mine_err, lat_t, decoder)
    dec_grad, lat_grad = last_gradients(row_set, other_err, other_t, decoder, parts, held)
    return recon[None], dec_grad[None], lat_grad[None]


def solution(mesh):
    return jax.shard_map(
        per_device,
        mesh=mesh,
        in_specs=(
            P("layer", "latent", None),
            P("layer", "latent", None),
            P("layer", None, "latent"),
            P("layer", "latent"),
            P("layer", None, "latent", None),
        ),
        out_specs=(
            P("layer", "latent", None),
            P("layer", None, "latent", None),
            P("layer", None, "latent"),
        ),
        check_vma=False,
    )
```

```python
import jax
import jax.numpy as jnp
from jax import lax
from jax.experimental import pallas as pl
from jax.experimental.pallas import tpu as pltpu
from jax.sharding import PartitionSpec as P

BF = jnp.bfloat16
F32 = jnp.float32


def place(z, y, rows):
    return 8 * z + 2 * y + ((rows ^ z ^ y) & 1)


ALONG_Z = [[place(z, y, r) for z in range(4)] for y in range(4) for r in range(2)]
ALONG_Y = [[place(z, y, r) for y in range(4)] for z in range(4) for r in range(2)]


def swap_cores(block):
    return lax.ppermute(block, "latent", [(i, i ^ 1) for i in range(32)])


def exchange_z(block, first, second):
    route = [
        (place(z, y, r), place(z ^ (second if r else first), y, r))
        for z in range(4)
        for y in range(4)
        for r in range(2)
    ]
    return lax.ppermute(block, "latent", route)


def shift_layer(block, distance):
    count = lax.axis_size("layer")
    route = [(i, i + distance) for i in range(count) if 0 <= i + distance < count]
    return lax.ppermute(block, "layer", route)


VMEM = pl.BlockSpec(memory_space=pltpu.VMEM)
ANYWHERE = pl.BlockSpec(memory_space=pl.ANY)
ACROSS = (((1,), (1,)), ((), ()))


def call(kernel, outs, specs, out_specs, flops, scratch=()):
    return pl.pallas_call(
        kernel,
        out_shape=outs,
        in_specs=specs,
        out_specs=out_specs,
        scratch_shapes=scratch,
        compiler_params=pltpu.CompilerParams(vmem_limit_bytes=32 * 1024 * 1024),
        cost_estimate=pl.CostEstimate(flops=flops, bytes_accessed=2_000_000, transcendentals=0),
    )


def pack_kernel(enc_ref, bias_ref, dec_ref, out_ref, bias_buf, sems):
    pairs = [(dec_ref.at[i, pl.ds(j, 128)], out_ref.at[pl.ds(384 * i + j, 128)]) for i in range(2) for j in (0, 128, 256)]
    pairs += [
        (enc_ref.at[pl.ds(512 * i + j, 256)], out_ref.at[pl.ds(768 + j, 256), pl.ds(384 * i, 384)])
        for i in range(2)
        for j in (0, 256)
    ]
    loads = [pltpu.make_async_copy(pair[0], pair[1], sems.at[i]) for i, pair in enumerate(pairs)]
    bias_load = pltpu.make_async_copy(bias_ref, bias_buf, sems.at[10])
    bias_load.start()
    for load in loads:
        load.start()
    bias_load.wait()
    rest = jnp.broadcast_to(bias_buf[...], (16, 384))
    row = lax.broadcasted_iota(jnp.int32, (16, 384), 0)
    rows = jnp.zeros((16, 384), F32)
    for i in range(3):
        piece = rest.astype(BF).astype(F32)
        rows = jnp.where(row == i, piece, rows)
        rest = rest - piece
    out_ref[1280:1296, 0:384] = rows.astype(BF)
    for load in loads:
        load.wait()


def pack(encoder, bias, decoder):
    out = jax.ShapeDtypeStruct((1296, 1024), BF)
    scratch = [pltpu.VMEM((1, 384), F32), pltpu.SemaphoreType.DMA((11,))]
    encoder, bias, decoder = (pltpu.with_memory_space_constraint(a, pltpu.HBM) for a in (encoder, bias, decoder))
    return call(pack_kernel, out, [ANYWHERE] * 3, VMEM, 1, scratch)(
        encoder, bias, decoder
    )


def forward_kernel(rows_ref, own_ref, sib_ref, part_ref, lat_ref, other_ref):
    def dot(a, b):
        return jnp.dot(a, b, preferred_element_type=F32)

    lats = []
    for from_ref, to_ref in ((own_ref, lat_ref), (sib_ref, other_ref)):
        pieces = from_ref[1280:1296, 0:384].astype(F32)
        lat = dot(rows_ref[:, 0:512], from_ref[768:1280, 0:384])
        lat += dot(rows_ref[:, 512:1024], from_ref[768:1280, 384:768])
        lat += pieces[0:1] + pieces[1:2] + pieces[2:3]
        lats.append(jnp.maximum(lat, 0.0).astype(BF))
        to_ref[...] = lats[-1]
    for s in range(2):
        decoder = slice(384 * s, 384 * (s + 1))
        total = dot(lats[0], own_ref[decoder, :]) + dot(lats[1], sib_ref[decoder, :])
        part_ref[:, :, 1024 * s : 1024 * (s + 1)] = total.astype(BF).reshape(4, 64, 1024)


def forward(rows, own, sibling):
    outs = (
        jax.ShapeDtypeStruct((4, 64, 2048), BF),
        jax.ShapeDtypeStruct((256, 384), BF),
        jax.ShapeDtypeStruct((256, 384), BF),
    )
    return call(forward_kernel, outs, [VMEM] * 3, (VMEM,) * 3, 1_207_959_552)(rows, own, sibling)


def copies_kernel(own_ref, next_ref, out_ref):
    for y in range(4):
        out_ref[y, 0] = own_ref[...]
        out_ref[y, 1] = next_ref[...]


def copies(own, after):
    out = jax.ShapeDtypeStruct((4, 2, 64, 1024), BF)
    return call(copies_kernel, out, [VMEM] * 2, VMEM, 1)(own, after)


def rows_of(err_ref, s):
    return err_ref[:, s].reshape(256, 1024)


def latent_rows(err_ref, dec_ref):
    total = lax.dot_general(rows_of(err_ref, 0), dec_ref[0], ACROSS, preferred_element_type=F32)
    total += lax.dot_general(rows_of(err_ref, 1), dec_ref[1], ACROSS, preferred_element_type=F32)
    return total.astype(BF)


def first_kernel(err_ref, lat_ref, dec_ref, parts_ref, held_ref):
    for s in range(2):
        parts_ref[s] = jnp.dot(lat_ref[...], rows_of(err_ref, s), preferred_element_type=F32)
    held_ref[...] = latent_rows(err_ref, dec_ref)


def first_gradients(err, lat_t, decoder):
    outs = (jax.ShapeDtypeStruct((2, 384, 1024), F32), jax.ShapeDtypeStruct((256, 384), BF))
    return call(first_kernel, outs, [VMEM] * 3, (VMEM, VMEM), 805_306_368)(err, lat_t, decoder)


def last_kernel(set_ref, err_ref, lat_ref, dec_ref, parts_ref, held_ref, dec_out, lat_out, dec_buf, lat_buf, sems):
    even = set_ref[0] * 16
    sends = [
        pltpu.make_async_copy(
            dec_buf.at[s, pl.ds(128 * i, 128)], dec_out.at[s, pl.ds(128 * i, 128)], sems.at[3 * s + i]
        )
        for s in range(2)
        for i in range(3)
    ]
    sends += [
        pltpu.make_async_copy(lat_buf.at[pl.ds(256 * i, 256)], lat_out.at[pl.ds(256 * i, 256)], sems.at[6 + i])
        for i in range(2)
    ]
    for s in range(2):
        total = parts_ref[s] + jnp.dot(lat_ref[...], rows_of(err_ref, s), preferred_element_type=F32)
        dec_buf[s] = total.astype(BF)
        for i in range(3):
            sends[3 * s + i].start()
    total = latent_rows(err_ref, dec_ref)
    for z in range(4):
        for y in range(4):
            here = y * 64 + z * 16
            there = z * 128 + y * 32
            at = even if (y ^ z) & 1 == 0 else 16 - even
            away = 16 - at
            lat_buf[pl.ds(pl.multiple_of(there + at, 16), 16), :] = held_ref[here : here + 16, :]
            lat_buf[pl.ds(pl.multiple_of(there + away, 16), 16), :] = total[here : here + 16, :]
        if z % 2:
            sends[6 + z // 2].start()
    for send in sends:
        send.wait()


def last_gradients(row_set, err, lat_t, decoder, parts, held):
    outs = (jax.ShapeDtypeStruct((2, 384, 1024), BF), jax.ShapeDtypeStruct((512, 384), BF))
    specs = [pl.BlockSpec(memory_space=pltpu.SMEM)] + [VMEM] * 5
    scratch = [pltpu.VMEM((2, 384, 1024), BF), pltpu.VMEM((512, 384), BF), pltpu.SemaphoreType.DMA((8,))]
    return call(last_kernel, outs, specs, (ANYWHERE, ANYWHERE), 805_306_368, scratch)(
        row_set.reshape(1), err, lat_t, decoder, parts, held
    )


def per_device(residual, targets, enc_weight, enc_bias, dec_weight):
    w_encode = enc_weight[0]
    decoder = dec_weight[0]
    target = targets[0].astype(F32)
    latent = lax.axis_index("latent")
    z_at = (latent // 8) * 16
    row_set = (latent ^ (latent // 2) ^ (latent // 8)) & 1

    packed = pack(w_encode, enc_bias, decoder)
    sibling = swap_cores(packed)

    mine = lax.all_gather(residual[0], "latent", axis=0, tiled=True, axis_index_groups=ALONG_Z)
    mine, sibling = lax.optimization_barrier((mine, sibling))
    mine = lax.all_gather(mine, "latent", axis=0, tiled=True, axis_index_groups=ALONG_Y)
    part, lat_mine, lat_sibling = forward(mine, packed, sibling)
    part = lax.all_to_all(part, "latent", 0, 0, tiled=True, axis_index_groups=ALONG_Y)
    part = jnp.sum(part.astype(F32), axis=0)
    shifted = shift_layer(part[:, 1024:].astype(BF), 1)
    shifted, lat_t, lat_sibling = lax.optimization_barrier((shifted, lat_mine.T, lat_sibling))
    part = part[:, :1024] + shifted.astype(F32)
    own = lax.dynamic_slice(part, (z_at, 0), (16, 1024)) - target
    part = lax.dynamic_update_slice(part, own, (z_at, 0))
    met, early = lax.optimization_barrier((exchange_z(part.astype(BF), 1, 3), swap_cores(lat_sibling[:128])))
    part = part + met.astype(F32)
    part, late = lax.optimization_barrier((part, lat_sibling[128:]))
    met, late = lax.optimization_barrier((exchange_z(part.astype(BF), 3, 1), swap_cores(late)))
    part = part + met.astype(F32)
    other_t = jnp.concatenate([early, late]).T
    recon = (lax.dynamic_slice(part, (z_at, 0), (16, 1024)) + target).astype(BF)

    error = (0.25 * part).astype(BF)
    after, recon, other_t = lax.optimization_barrier((shift_layer(error, -1), recon, other_t))
    both = copies(error, after)
    mine_err = lax.all_to_all(both, "latent", 0, 0, tiled=True, axis_index_groups=ALONG_Y)
    other_err = swap_cores(mine_err)
    parts, held = first_gradients(mine_err, lat_t, decoder)
    dec_grad, lat_grad = last_gradients(row_set, other_err, other_t, decoder, parts, held)
    return recon[None], dec_grad[None], lat_grad[None]


def solution(mesh):
    return jax.shard_map(
        per_device,
        mesh=mesh,
        in_specs=(
            P("layer", "latent", None),
            P("layer", "latent", None),
            P("layer", None, "latent"),
            P("layer", "latent"),
            P("layer", None, "latent", None),
        ),
        out_specs=(
            P("layer", "latent", None),
            P("layer", None, "latent", None),
            P("layer", None, "latent"),
        ),
        check_vma=False,
    )
```

```python
import jax
import jax.numpy as jnp
from jax import lax
from jax.experimental import pallas as pl
from jax.experimental.pallas import tpu as pltpu
from jax.sharding import PartitionSpec as P

BF = jnp.bfloat16
F32 = jnp.float32


def place(z, y, rows):
    return 8 * z + 2 * y + ((rows ^ z ^ y) & 1)


ALONG_Z = [[place(z, y, r) for z in range(4)] for y in range(4) for r in range(2)]
ALONG_Y = [[place(z, y, r) for y in range(4)] for z in range(4) for r in range(2)]


def swap_cores(block):
    return lax.ppermute(block, "latent", [(i, i ^ 1) for i in range(32)])


def exchange_z(block, first, second):
    route = [
        (place(z, y, r), place(z ^ (second if r else first), y, r))
        for z in range(4)
        for y in range(4)
        for r in range(2)
    ]
    return lax.ppermute(block, "latent", route)


def shift_layer(block, distance):
    count = lax.axis_size("layer")
    route = [(i, i + distance) for i in range(count) if 0 <= i + distance < count]
    return lax.ppermute(block, "layer", route)


VMEM = pl.BlockSpec(memory_space=pltpu.VMEM)
ANYWHERE = pl.BlockSpec(memory_space=pl.ANY)
ACROSS = (((1,), (1,)), ((), ()))


def call(kernel, outs, specs, out_specs, flops, scratch=()):
    return pl.pallas_call(
        kernel,
        out_shape=outs,
        in_specs=specs,
        out_specs=out_specs,
        scratch_shapes=scratch,
        compiler_params=pltpu.CompilerParams(vmem_limit_bytes=32 * 1024 * 1024),
        cost_estimate=pl.CostEstimate(flops=flops, bytes_accessed=2_000_000, transcendentals=0),
    )


def pack_kernel(enc_ref, bias_ref, dec_ref, out_ref, bias_buf, sems):
    pairs = [(dec_ref.at[i, pl.ds(j, 128)], out_ref.at[pl.ds(384 * i + j, 128)]) for i in range(2) for j in (0, 128, 256)]
    pairs += [
        (enc_ref.at[pl.ds(512 * i + j, 256)], out_ref.at[pl.ds(768 + j, 256), pl.ds(384 * i, 384)])
        for i in range(2)
        for j in (0, 256)
    ]
    loads = [pltpu.make_async_copy(pair[0], pair[1], sems.at[i]) for i, pair in enumerate(pairs)]
    bias_load = pltpu.make_async_copy(bias_ref, bias_buf, sems.at[10])
    bias_load.start()
    for load in loads:
        load.start()
    bias_load.wait()
    rest = jnp.broadcast_to(bias_buf[...], (16, 384))
    row = lax.broadcasted_iota(jnp.int32, (16, 384), 0)
    rows = jnp.zeros((16, 384), F32)
    for i in range(3):
        piece = rest.astype(BF).astype(F32)
        rows = jnp.where(row == i, piece, rows)
        rest = rest - piece
    out_ref[1280:1296, 0:384] = rows.astype(BF)
    for load in loads:
        load.wait()


def pack(encoder, bias, decoder):
    out = jax.ShapeDtypeStruct((1296, 1024), BF)
    scratch = [pltpu.VMEM((1, 384), F32), pltpu.SemaphoreType.DMA((11,))]
    encoder, bias, decoder = (pltpu.with_memory_space_constraint(a, pltpu.HBM) for a in (encoder, bias, decoder))
    return call(pack_kernel, out, [ANYWHERE] * 3, VMEM, 1, scratch)(
        encoder, bias, decoder
    )


def forward_kernel(rows_ref, own_ref, sib_ref, part_ref, lat_ref, other_ref):
    def dot(a, b):
        return jnp.dot(a, b, preferred_element_type=F32)

    lats = []
    for from_ref, to_ref in ((own_ref, lat_ref), (sib_ref, other_ref)):
        pieces = from_ref[1280:1296, 0:384].astype(F32)
        lat = dot(rows_ref[:, 0:512], from_ref[768:1280, 0:384])
        lat += dot(rows_ref[:, 512:1024], from_ref[768:1280, 384:768])
        lat += pieces[0:1] + pieces[1:2] + pieces[2:3]
        lats.append(jnp.maximum(lat, 0.0).astype(BF))
        to_ref[...] = lats[-1]
    for s in range(2):
        decoder = slice(384 * s, 384 * (s + 1))
        total = dot(lats[0], own_ref[decoder, :]) + dot(lats[1], sib_ref[decoder, :])
        part_ref[:, :, 1024 * s : 1024 * (s + 1)] = total.astype(BF).reshape(4, 64, 1024)


def forward(rows, own, sibling):
    outs = (
        jax.ShapeDtypeStruct((4, 64, 2048), BF),
        jax.ShapeDtypeStruct((256, 384), BF),
        jax.ShapeDtypeStruct((256, 384), BF),
    )
    return call(forward_kernel, outs, [VMEM] * 3, (VMEM,) * 3, 1_207_959_552)(rows, own, sibling)


def copies_kernel(own_ref, next_ref, out_ref):
    for y in range(4):
        out_ref[y, 0] = own_ref[...]
        out_ref[y, 1] = next_ref[...]


def copies(own, after):
    out = jax.ShapeDtypeStruct((4, 2, 64, 1024), BF)
    return call(copies_kernel, out, [VMEM] * 2, VMEM, 1)(own, after)


def rows_of(err_ref, s):
    return err_ref[:, s].reshape(256, 1024)


def latent_rows(err_ref, dec_ref):
    total = lax.dot_general(rows_of(err_ref, 0), dec_ref[0], ACROSS, preferred_element_type=F32)
    total += lax.dot_general(rows_of(err_ref, 1), dec_ref[1], ACROSS, preferred_element_type=F32)
    return total.astype(BF)


def first_kernel(err_ref, lat_ref, dec_ref, parts_ref, held_ref):
    for s in range(2):
        parts_ref[s] = jnp.dot(lat_ref[...], rows_of(err_ref, s), preferred_element_type=F32)
    held_ref[...] = latent_rows(err_ref, dec_ref)


def first_gradients(err, lat_t, decoder):
    outs = (jax.ShapeDtypeStruct((2, 384, 1024), F32), jax.ShapeDtypeStruct((256, 384), BF))
    return call(first_kernel, outs, [VMEM] * 3, (VMEM, VMEM), 805_306_368)(err, lat_t, decoder)


def last_kernel(set_ref, err_ref, lat_ref, dec_ref, parts_ref, held_ref, dec_out, lat_out, dec_buf, lat_buf, sems):
    even = set_ref[0] * 16
    sends = [
        pltpu.make_async_copy(
            dec_buf.at[s, pl.ds(128 * i, 128)], dec_out.at[s, pl.ds(128 * i, 128)], sems.at[3 * s + i]
        )
        for s in range(2)
        for i in range(3)
    ]
    sends += [
        pltpu.make_async_copy(lat_buf.at[pl.ds(256 * i, 256)], lat_out.at[pl.ds(256 * i, 256)], sems.at[6 + i])
        for i in range(2)
    ]
    total = latent_rows(err_ref, dec_ref)
    for z in range(4):
        for y in range(4):
            here = y * 64 + z * 16
            there = z * 128 + y * 32
            at = even if (y ^ z) & 1 == 0 else 16 - even
            away = 16 - at
            lat_buf[pl.ds(pl.multiple_of(there + at, 16), 16), :] = held_ref[here : here + 16, :]
            lat_buf[pl.ds(pl.multiple_of(there + away, 16), 16), :] = total[here : here + 16, :]
        if z % 2:
            sends[6 + z // 2].start()
    for s in range(2):
        total = parts_ref[s] + jnp.dot(lat_ref[...], rows_of(err_ref, s), preferred_element_type=F32)
        dec_buf[s] = total.astype(BF)
        for i in range(3):
            sends[3 * s + i].start()
    for send in sends:
        send.wait()


def last_gradients(row_set, err, lat_t, decoder, parts, held):
    outs = (jax.ShapeDtypeStruct((2, 384, 1024), BF), jax.ShapeDtypeStruct((512, 384), BF))
    specs = [pl.BlockSpec(memory_space=pltpu.SMEM)] + [VMEM] * 5
    scratch = [pltpu.VMEM((2, 384, 1024), BF), pltpu.VMEM((512, 384), BF), pltpu.SemaphoreType.DMA((8,))]
    return call(last_kernel, outs, specs, (ANYWHERE, ANYWHERE), 805_306_368, scratch)(
        row_set.reshape(1), err, lat_t, decoder, parts, held
    )


def per_device(residual, targets, enc_weight, enc_bias, dec_weight):
    w_encode = enc_weight[0]
    decoder = dec_weight[0]
    target = targets[0].astype(F32)
    latent = lax.axis_index("latent")
    z_at = (latent // 8) * 16
    row_set = (latent ^ (latent // 2) ^ (latent // 8)) & 1

    packed = pack(w_encode, enc_bias, decoder)
    sibling = swap_cores(packed)

    mine = lax.all_gather(residual[0], "latent", axis=0, tiled=True, axis_index_groups=ALONG_Z)
    mine, sibling = lax.optimization_barrier((mine, sibling))
    mine = lax.all_gather(mine, "latent", axis=0, tiled=True, axis_index_groups=ALONG_Y)
    part, lat_mine, lat_sibling = forward(mine, packed, sibling)
    part = lax.all_to_all(part, "latent", 0, 0, tiled=True, axis_index_groups=ALONG_Y)
    part = jnp.sum(part.astype(F32), axis=0)
    shifted = shift_layer(part[:, 1024:].astype(BF), 1)
    shifted, lat_t, lat_sibling = lax.optimization_barrier((shifted, lat_mine.T, lat_sibling))
    part = part[:, :1024] + shifted.astype(F32)
    own = lax.dynamic_slice(part, (z_at, 0), (16, 1024)) - target
    part = lax.dynamic_update_slice(part, own, (z_at, 0))
    halves = [swap_cores(lat_sibling[:128]), swap_cores(lat_sibling[128:])]
    met, *halves = lax.optimization_barrier((exchange_z(part.astype(BF), 1, 3), *halves))
    other_t = jnp.concatenate(halves).T
    part = part + met.astype(F32)
    part = part + exchange_z(part.astype(BF), 3, 1).astype(F32)
    recon = (lax.dynamic_slice(part, (z_at, 0), (16, 1024)) + target).astype(BF)

    error = (0.25 * part).astype(BF)
    after, recon, other_t = lax.optimization_barrier((shift_layer(error, -1), recon, other_t))
    both = copies(error, after)
    mine_err = lax.all_to_all(both, "latent", 0, 0, tiled=True, axis_index_groups=ALONG_Y)
    other_err = swap_cores(mine_err)
    parts, held = first_gradients(mine_err, lat_t, decoder)
    dec_grad, lat_grad = last_gradients(row_set, other_err, other_t, decoder, parts, held)
    return recon[None], dec_grad[None], lat_grad[None]


def solution(mesh):
    return jax.shard_map(
        per_device,
        mesh=mesh,
        in_specs=(
            P("layer", "latent", None),
            P("layer", "latent", None),
            P("layer", None, "latent"),
            P("layer", "latent"),
            P("layer", None, "latent", None),
        ),
        out_specs=(
            P("layer", "latent", None),
            P("layer", None, "latent", None),
            P("layer", None, "latent"),
        ),
        check_vma=False,
    )
```
